32 devices in a mesh: groups: 2 (over y), adapt: 8 (over z, core), tensor: 2 (over x).
Axes of the slice: x: 2, y: 2, z: 4, core: 2. Of those that a mesh axis runs over, the one named last changes fastest.
Arguments:
- hidden: bfloat16 [512, 8192], P(('groups', 'adapt'), 'tensor'), parts along dimension 0, may hold values from -6 to 6
- queries: bfloat16 [512, 8192], P(('groups', 'adapt'), 'tensor'), parts along dimension 0, may hold values from -5 to 5
- key_value_cache: bfloat16 [512, 2, 512, 1024], P(('groups', 'adapt'), None, None, 'tensor'), parts along dimension 0, may hold values from -4 to 4
- key_value_weight: bfloat16 [8192, 2, 1024], P(None, None, 'tensor'), may hold values from -0.0625 to 0.0625
- adapter_down_weight: bfloat16 [8, 8192, 128], P('adapt', 'tensor'), may hold values from -0.0625 to 0.0625
- adapter_up_weight: bfloat16 [8, 2, 64, 1024], P('adapt', None, None, 'tensor'), may hold values from -0.75 to 0.75
- request_adapter_index: int32 [512, 1], P(('groups', 'adapt')), parts along dimension 0, may hold values from 0 to 7; in each aligned block of 32 rows (0 to 31, 32 to 63, ...) at most 4 rows name the same one
- lengths: int32 [512], P(('groups', 'adapt')), parts along dimension 0, may hold values from 2 to 512, as said below
Outputs:
- attention: bfloat16 [512, 8192], P(('groups', 'adapt'), 'tensor'), parts along dimension 0
- new_entries: bfloat16 [512, 2, 1024], P(('groups', 'adapt'), None, 'tensor'), parts along dimension 0
The draws below stay inside these ranges and needn't reach their ends.
There are 2 independent parts, one for each index of `groups`. The reference program is written for one: setup_inputs(seed, part) draws one part's arguments, and reference() takes and returns one part's arrays. A program takes and returns all parts, laid end to end along the dimension named above; an argument that names none is the same for every part. Nothing has to cross between parts.
Inputs may be any that keep to these rules, and one draw needn't show every extreme that they name: `request_adapter_index`: every adapter is named by some request; among the 32 requests of one device no adapter is named more than 4 times, a bound that some block reaches. `lengths`: some request of every device has all 512 positions valid.
All inputs are finite; a program needn't handle non-finite values.
Results may differ from the reference program's by a relative error of at most 0.015.
Values may be sent and summed in bfloat16 or wider, within the bound.
A program may use at most 192 MiB of HBM per device.

```python
import math
import jax
import jax.numpy as jnp
import numpy as np
from jax import lax

MODEL_WIDTH = 8192
HEAD_DIM = 128
Q_HEADS = 64
KV_HEADS = 8
ADAPTER_RANK = 64
MOST = 4
REQ_DEV = 32
CTX = 512
REQUESTS = 256
ADAPTER_COUNT = 8
KEY_FEATURES = 1024
GROUP = 8


def draw_queries(key, part):
    key = jax.random.fold_in(key, 11)
    output_shape = (REQUESTS, KV_HEADS, GROUP, HEAD_DIM)
    values = jnp.clip(jax.random.normal(key, output_shape, jnp.float32), -4.0, 4.0)
    return values.reshape(REQUESTS, KV_HEADS * GROUP * HEAD_DIM).astype(jnp.bfloat16)


def draw_key_value_cache(key, part):
    key = jax.random.fold_in(key, 12)
    output_shape = (REQUESTS, 2, CTX, KV_HEADS, HEAD_DIM)
    values = jnp.clip(jax.random.normal(key, output_shape, jnp.float32), -4.0, 4.0)
    return values.reshape(REQUESTS, 2, CTX, KV_HEADS * HEAD_DIM).astype(jnp.bfloat16)


def draw_lengths(key, part):
    key = jax.random.fold_in(key, 13)
    first_key, second_key, third_key, fourth_key = jax.random.split(key, 4)
    longer = jax.random.randint(first_key, (REQUESTS,), 2, CTX + 1)
    shorter = jax.random.randint(second_key, (REQUESTS,), 2, CTX // 8 + 3)
    which = jax.random.randint(third_key, (REQUESTS,), 0, 2)
    spans = jnp.where(which == 0, shorter, longer)
    filled = jax.random.randint(fourth_key, (REQUESTS // REQ_DEV,), 0, REQ_DEV)
    marks = jnp.repeat(filled, REQ_DEV)
    spans = jnp.where(jnp.arange(REQUESTS) % REQ_DEV == marks, CTX, spans)
    return spans.astype(jnp.int32)


def block_scale(own_key, shape, shards, low, top_value):
    def one(axis_at, blocks):
        steps = jax.random.uniform(jax.random.fold_in(jax.random.fold_in(own_key, 6), axis_at), (blocks,), jnp.float32, low / len(shards), top_value / len(shards))
        return jnp.repeat(jnp.exp(steps), shape[axis_at] // blocks).reshape((-1,) + (1,) * (len(shape) - axis_at - 1))

    gain = one(*shards[0])
    for cut in shards[1:]:
        gain = gain * one(*cut)
    return gain


def assign_block(rng, own, number, rows, amount, top, limit, slope):
    ranking = jax.random.permutation(rng, amount)
    crowded, common = shares(amount, rows * top, limit, slope, True), shares(amount, rows * top, limit, slope, False)
    places = jnp.arange(amount)

    def named(sizes, turn):
        used = int((sizes > 0).sum())
        fixed = max(1, used // 4)
        moved = fixed + (places - fixed + turn * (used - fixed)) % max(1, amount - fixed)
        return jnp.zeros((amount,), jnp.int32).at[ranking[jnp.where(places < fixed, places, moved)]].set(jnp.asarray(sizes, jnp.int32))

    sizes = jnp.where(number % 4 == 0, named(crowded, number // 4), named(common, number - number // 4 - 1))
    mixed = jax.random.permutation(jax.random.fold_in(own, 3), amount)
    donor, taker = mixed[0:amount // 2 * 2:2], mixed[1:amount // 2 * 2:2]
    room = jnp.minimum(sizes[donor] - 1, limit - sizes[taker]) // 2
    room = jnp.where((donor == ranking[0]) | (taker == ranking[0]) | (sizes[taker] == 0), 0, jnp.maximum(room, 0))
    moved = jax.random.randint(jax.random.fold_in(own, 4), (amount // 2,), 0, 1 << 20) % (room + 1)
    sizes = sizes.at[donor].add(-moved).at[taker].add(moved)
    members = jnp.searchsorted(jnp.cumsum(sizes), jnp.arange(rows * top), side="right").astype(jnp.int32)
    table = members.reshape(top, rows).T
    table = table[jax.random.permutation(jax.random.fold_in(own, 1), rows)]
    turn = jax.random.randint(jax.random.fold_in(own, 2), (rows, 1), 0, top)
    return jnp.take_along_axis(table, (jnp.arange(top)[None, :] + turn) % top, axis=1)


def shares(number_of, total, most, slope, full):
    weights = [(1 << 20) // math.isqrt(standing ** slope) + 1 for standing in range(1, number_of + 1)]
    largest = most if full else min(most, max(-(-total // number_of), total * weights[0] // sum(weights)))
    least = 1 if total - largest >= number_of - 1 else 0
    counts, surplus = [largest] + [least] * (number_of - 1), total - largest - least * (number_of - 1)
    while surplus > 0:
        movable = [i for i in range(1, number_of) if counts[i] < largest] or [i for i in range(1, number_of) if counts[i] < most]
        whole, budget = sum([weights[i] for i in movable]), surplus
        for i in movable:
            addition = min(most - counts[i], max(1, budget * weights[i] // whole), surplus)
            counts[i] = counts[i] + addition
            surplus = surplus - addition
    return np.array(counts)


def scatter_about(rng, dims, scale, bound, cuts=(), kind=jnp.bfloat16):
    values = scale * jax.random.normal(rng, dims, jnp.float32)
    if cuts:
        values = values * block_scale(rng, dims, cuts, -0.22, 0.18)
    return jnp.clip(values, -bound, bound).astype(kind)


def setup_inputs(seed: int = 0, part: int = 0) -> dict:
    seeds = jax.random.split(jax.random.key(seed), 9)
    part_splits = jax.random.split(jax.random.fold_in(seeds[8], part), 9)
    hidden = scatter_about(part_splits[0], (REQUESTS, MODEL_WIDTH), 1.0, 6.0, ((0, 8), (1, 2)))
    queries = draw_queries(jax.random.fold_in(jax.random.fold_in(seeds[8], part), 71), part)
    key_value_cache = draw_key_value_cache(jax.random.fold_in(jax.random.fold_in(seeds[8], part), 71), part)
    key_value_weight = scatter_about(seeds[3], (MODEL_WIDTH, 2, KEY_FEATURES), MODEL_WIDTH ** -0.5, 0.0625, ((2, 2),))
    adapter_down_weight = scatter_about(seeds[4], (ADAPTER_COUNT, MODEL_WIDTH, 2 * ADAPTER_RANK), MODEL_WIDTH ** -0.5, 0.0625, ((0, 8), (1, 2)))
    adapter_up_weight = scatter_about(seeds[5], (ADAPTER_COUNT, 2, ADAPTER_RANK, KEY_FEATURES), ADAPTER_RANK ** -0.5, 0.75, ((0, 8), (3, 2)))
    request_adapter_index_keys = jax.random.split(jax.random.fold_in(part_splits[6], 1), REQUESTS // REQ_DEV)
    request_adapter_index_turns = jax.random.permutation(jax.random.fold_in(part_splits[6], 3), REQUESTS // REQ_DEV)
    request_adapter_index = jax.vmap(lambda own, number: assign_block(jax.random.fold_in(part_splits[6], 2), own, number, REQ_DEV, ADAPTER_COUNT, 1, MOST, 2))(request_adapter_index_keys, request_adapter_index_turns).reshape((REQUESTS, 1))
    lengths = draw_lengths(jax.random.fold_in(jax.random.fold_in(seeds[8], part), 71), part)
    return dict(hidden=hidden, queries=queries, key_value_cache=key_value_cache, key_value_weight=key_value_weight, adapter_down_weight=adapter_down_weight, adapter_up_weight=adapter_up_weight, request_adapter_index=request_adapter_index, lengths=lengths)


ADAPTER_SCALE = 2.0
THETA = 500000.0

def rotary(fields, positions):
    half_dim = HEAD_DIM // 2
    freqs = THETA ** (-(jnp.arange(half_dim, dtype=jnp.float32) * 2.0) / HEAD_DIM)
    angles = positions.astype(jnp.float32)[:, None] * freqs[None, :]
    cosine = jnp.cos(angles)[:, None, :]
    sine = jnp.sin(angles)[:, None, :]
    first_half = fields[..., :half_dim]
    second_half = fields[..., half_dim:]
    return jnp.concatenate([first_half * cosine - second_half * sine, second_half * cosine + first_half * sine], -1)

def attend_one(packed):
    query_row, cache_row, entry_row, length = packed
    query_heads = query_row.reshape(KV_HEADS, GROUP, HEAD_DIM).astype(jnp.float32)
    cached_keys = cache_row[0].reshape(CTX, KV_HEADS, HEAD_DIM).astype(jnp.float32)
    cached_values = cache_row[1].reshape(CTX, KV_HEADS, HEAD_DIM).astype(jnp.float32)
    fresh_key = entry_row[0].reshape(KV_HEADS, HEAD_DIM).astype(jnp.float32)
    fresh_value = entry_row[1].reshape(KV_HEADS, HEAD_DIM).astype(jnp.float32)
    scaling = 1.0 / jnp.sqrt(jnp.float32(HEAD_DIM))
    scores = jnp.einsum('gih,pgh->gip', query_heads, cached_keys) * scaling
    own_score = jnp.einsum('gih,gh->gi', query_heads, fresh_key) * scaling
    valid = (jnp.arange(CTX) < length)[None, None, :]
    scores = jnp.where(valid, scores, jnp.float32(-1e+30))
    highest = jnp.maximum(lax.optimization_barrier(jnp.max(scores, -1)), own_score)
    weights = jnp.where(valid, jnp.exp(scores - highest[..., None]), jnp.float32(0.0))
    own_weight = jnp.exp(own_score - highest)
    totals = lax.optimization_barrier(jnp.sum(weights, -1)) + own_weight
    probs = (weights / totals[..., None]).astype(jnp.bfloat16).astype(jnp.float32)
    own_prob = (own_weight / totals).astype(jnp.bfloat16).astype(jnp.float32)
    mixed = jnp.einsum('gip,pgh->gih', probs, cached_values) + own_prob[..., None] * fresh_value[:, None, :]
    return mixed.reshape(Q_HEADS * HEAD_DIM).astype(jnp.bfloat16)

def reference(hidden, queries, key_value_cache, key_value_weight, adapter_down_weight, adapter_up_weight, request_adapter_index, lengths):
    picked_adapter_index = request_adapter_index[:, 0]
    base = jnp.dot(hidden, key_value_weight.reshape(MODEL_WIDTH, 2 * KEY_FEATURES), preferred_element_type=jnp.float32).reshape(REQUESTS, 2, KEY_FEATURES)
    all_reduced_inputs = jnp.einsum('zf,qfv->zqv', hidden.astype(jnp.float32), adapter_down_weight.astype(jnp.float32))
    one_hot = (picked_adapter_index[:, None] == jnp.arange(ADAPTER_COUNT, dtype=jnp.int32)[None, :]).astype(jnp.float32)
    shrunk = jnp.einsum('rac,ra->rc', all_reduced_inputs, one_hot).astype(jnp.bfloat16)
    chosen_up_weight = adapter_up_weight[picked_adapter_index].astype(jnp.float32)
    adapter_update = jnp.einsum('rtc,rtcx->rtx', shrunk.reshape(REQUESTS, 2, ADAPTER_RANK).astype(jnp.float32), chosen_up_weight)
    adapter_update = (ADAPTER_SCALE * adapter_update).astype(jnp.bfloat16)
    fresh = base + adapter_update.astype(jnp.float32)
    keys = rotary(fresh[:, 0].reshape(REQUESTS, KV_HEADS, HEAD_DIM), lengths).reshape(REQUESTS, KEY_FEATURES)
    new_entries = jnp.stack([keys, fresh[:, 1]], 1).astype(jnp.bfloat16)
    attention = lax.map(attend_one, (queries, key_value_cache, new_entries, lengths))
    return (attention, new_entries)
```

```python
import functools

import jax
import jax.numpy as jnp
from jax import lax
from jax.experimental import pallas as pl
from jax.experimental.pallas import tpu as pltpu
from jax.sharding import PartitionSpec as P

HEAD_DIM = 128
GROUP = 8
MOST = 4
ADAPTER_SCALE = 2.0
THETA = 500000.0
ROWS = 16
CUT = ROWS // MOST
DEPTH = 512
SLOTS = 4
CHUNK = 128
AHEAD = 8
MESH = pl.DeviceIdType.MESH
F32 = jnp.float32
BF16 = jnp.bfloat16


def one_hot(condition):
    return jnp.where(condition, 1.0, 0.0).astype(BF16)


def iota(shape, dim):
    return lax.broadcasted_iota(jnp.int32, shape, dim)


def entries_kernel(
    adapters, tensors,
    hidden, weight, down, up, index_col, index_row, cosine, sine, out,
    blocks, wide, gathered, sent, taken, partial, back_sent, back, down_here, up_here, total,
    block_sem, local_sem, hs, hr, ds, dr, ps, pr, rs, rr,
):
    me = lax.axis_index("adapt")
    side = lax.axis_index("tensor")
    rows, local = hidden.shape
    cols = out.shape[2]
    tiles = cols // 128
    per_source = local // DEPTH
    count = per_source * tensors
    piece = local // CUT

    def block_copies(n):
        source = lax.rem(side + tensors - n // per_source, tensors)
        start = pl.multiple_of(source * local + lax.rem(n, per_source) * DEPTH, DEPTH)
        slot = lax.rem(n, SLOTS)
        return [
            pltpu.make_async_copy(
                weight.at[pl.ds(start, DEPTH), :, pl.ds(tile * 128, 128)],
                blocks.at[slot, tile],
                block_sem.at[slot, tile],
            )
            for tile in range(tiles)
        ]

    down_copy = pltpu.make_async_copy(down.at[0], down_here, local_sem.at[0])
    up_copy = pltpu.make_async_copy(up.at[0], up_here, local_sem.at[1])

    barrier = pltpu.get_barrier_semaphore()
    for j in range(1, adapters):
        pl.semaphore_signal(
            barrier, inc=1, device_id={"adapt": lax.rem(me + j, adapters)}, device_id_type=MESH
        )
    for j in range(1, tensors):
        pl.semaphore_signal(
            barrier, inc=1, device_id={"tensor": lax.rem(side + j, tensors)}, device_id_type=MESH
        )
    for n in range(SLOTS):
        for copy in block_copies(jnp.int32(n)):
            copy.start()
    down_copy.start()
    up_copy.start()

    col = index_col[...]
    row = index_row[...]
    same = col == row
    first, second = iota((rows, rows), 0), iota((rows, rows), 1)
    place_col = jnp.sum(jnp.where(same & (second < first), 1.0, 0.0), axis=1, keepdims=True)
    place_row = jnp.sum(jnp.where(same & (first < second), 1.0, 0.0), axis=0, keepdims=True)
    place_col = place_col.astype(jnp.int32)
    place_row = place_row.astype(jnp.int32)

    high = adapters * ROWS
    line = iota((high, rows), 0)
    wanted = (line // ROWS == row) & (line % MOST == place_row)
    packed = jnp.zeros((high, piece), F32)
    for q in range(CUT):
        pick = one_hot(wanted & (line % ROWS // MOST == q))
        packed += jnp.dot(
            pick, hidden[:, q * piece : (q + 1) * piece], preferred_element_type=F32
        )
    sent[...] = packed.astype(BF16)
    here = pl.ds(pl.multiple_of(me * ROWS, ROWS), ROWS)

    pl.semaphore_wait(barrier, adapters - 1 + tensors - 1)

    def block_of(j):
        return pl.ds(pl.multiple_of(lax.rem(me + j, adapters) * ROWS, ROWS), ROWS)

    out_copies, back_copies = [None], [None]
    for j in range(1, adapters):
        copy = pltpu.make_async_remote_copy(
            src_ref=sent.at[block_of(j)],
            dst_ref=taken.at[here],
            send_sem=ds.at[j],
            recv_sem=dr.at[j],
            device_id={"adapt": lax.rem(me + j, adapters)},
            device_id_type=MESH,
        )
        copy.start()
        out_copies.append(copy)
    hidden_copies, sum_copies = [None], [None]
    for j in range(1, tensors):
        copy = pltpu.make_async_remote_copy(
            src_ref=hidden,
            dst_ref=gathered.at[j],
            send_sem=hs.at[j],
            recv_sem=hr.at[j],
            device_id={"tensor": lax.rem(side + j, tensors)},
            device_id_type=MESH,
        )
        copy.start()
        hidden_copies.append(copy)
    taken[here] = sent[here]
    total[...] = jnp.zeros_like(total)

    spread = iota((128, 256), 1) - 2 * iota((128, 256), 0)
    even, odd = one_hot(spread == 0), one_hot(spread == 1)

    def widen(source):
        for at in range(local // 128):
            part = source[:, at * 128 : (at + 1) * 128]
            to = slice(at * 256, (at + 1) * 256)
            wide[:rows, to] = jnp.dot(part, even, preferred_element_type=F32).astype(BF16)
            wide[rows:, to] = jnp.dot(part, odd, preferred_element_type=F32).astype(BF16)

    def stream(low, top):
        def step(n, carry):
            slot = lax.rem(n, SLOTS)
            start = pl.multiple_of(lax.rem(n, per_source) * 2 * DEPTH, 2 * DEPTH)
            features = wide[:, pl.ds(start, 2 * DEPTH)]
            for tile, copy in enumerate(block_copies(n)):
                copy.wait()
                total[:, tile * 128 : (tile + 1) * 128] += jnp.dot(
                    features,
                    blocks.at[slot, tile].reshape(2 * DEPTH, 128)[...],
                    preferred_element_type=F32,
                )

            @pl.when(n + SLOTS < count)
            def _():
                for copy in block_copies(n + SLOTS):
                    copy.start()

            return carry

        lax.fori_loop(low, top, step, 0)

    widen(hidden)
    stream(0, per_source)

    for j in range(1, adapters):
        out_copies[j].wait_recv()
    down_copy.wait()
    arrived = taken[...]
    which = iota((high, 128), 0) % ROWS // MOST
    grown = jnp.zeros((high, 128), F32)
    for q in range(CUT):
        product = jnp.dot(
            arrived, down_here[q * piece : (q + 1) * piece, :], preferred_element_type=F32
        )
        grown = jnp.where(which == q, product, grown)
    short = adapters * MOST
    to, fro = iota((short, high), 0), iota((short, high), 1)
    fold = (to // MOST == fro // ROWS) & (to % MOST == fro % MOST)
    partial[0] = jnp.dot(
        jnp.where(fold, 1.0, 0.0), grown,
        preferred_element_type=F32, precision=lax.Precision.HIGHEST,
    )
    for j in range(1, tensors):
        copy = pltpu.make_async_remote_copy(
            src_ref=partial.at[0],
            dst_ref=partial.at[j],
            send_sem=ps.at[j],
            recv_sem=pr.at[j],
            device_id={"tensor": lax.rem(side + j, tensors)},
            device_id_type=MESH,
        )
        copy.start()
        sum_copies.append(copy)

    hidden_copies[1].wait_recv()
    widen(gathered.at[1])
    middle = per_source + per_source // 2
    stream(per_source, middle)

    up_copy.wait()
    rank_sum = partial[0]
    for j in range(1, tensors):
        sum_copies[j].wait_recv()
        rank_sum = rank_sum + partial[j]
    shrunk = rank_sum.astype(BF16)
    half = up_here.shape[1]
    to, fro = iota((high, short), 0), iota((high, short), 1)
    returned = jnp.zeros((high, cols), F32)
    for t in range(2):
        raised = jnp.dot(
            shrunk[:, t * half : (t + 1) * half], up_here[t], preferred_element_type=F32
        )
        raised = (ADAPTER_SCALE * raised).astype(BF16)
        put = (to // ROWS == fro // MOST) & (to % ROWS == fro % MOST + t * MOST)
        returned += jnp.dot(one_hot(put), raised, preferred_element_type=F32)
    back_sent[...] = returned.astype(BF16)
    for j in range(1, adapters):
        copy = pltpu.make_async_remote_copy(
            src_ref=back_sent.at[block_of(j)],
            dst_ref=back.at[here],
            send_sem=rs.at[j],
            recv_sem=rr.at[j],
            device_id={"adapt": lax.rem(me + j, adapters)},
            device_id_type=MESH,
        )
        copy.start()
        back_copies.append(copy)
    back[here] = back_sent[here]

    stream(middle, 2 * per_source)
    for j in range(2, tensors):
        hidden_copies[j].wait_recv()
        widen(gathered.at[j])
        stream(j * per_source, (j + 1) * per_source)

    for j in range(1, adapters):
        back_copies[j].wait_recv()
    updates = back[...]
    line = iota((rows, high), 1)
    for t in range(2):
        choose = one_hot((line // ROWS == col) & (line % ROWS == place_col + t * MOST))
        fresh = total[t * rows : (t + 1) * rows, :] + jnp.dot(
            choose, updates, preferred_element_type=F32
        )
        for head in range(cols // HEAD_DIM):
            at = slice(head * HEAD_DIM, (head + 1) * HEAD_DIM)
            part = fresh[:, at]
            if t == 0:
                part = part * cosine[...] + pltpu.roll(part, HEAD_DIM // 2, 1) * sine[...]
            out[t, :, at] = part.astype(BF16).astype(F32)

    for j in range(1, adapters):
        out_copies[j].wait_send()
        back_copies[j].wait_send()
    for j in range(1, tensors):
        hidden_copies[j].wait_send()
        sum_copies[j].wait_send()


def entries_of(adapters, tensors, hidden, weight, down, up, index, cosine, sine):
    rows, local = hidden.shape
    cols = weight.shape[2]
    high = adapters * ROWS
    dma = pltpu.SemaphoreType.DMA
    vmem = pl.BlockSpec(memory_space=pltpu.VMEM)
    hbm = pl.BlockSpec(memory_space=pl.ANY)
    return pl.pallas_call(
        functools.partial(entries_kernel, adapters, tensors),
        out_shape=jax.ShapeDtypeStruct((2, rows, cols), F32),
        in_specs=[vmem, hbm, hbm, hbm, vmem, vmem, vmem, vmem],
        out_specs=vmem,
        scratch_shapes=[
            pltpu.VMEM((SLOTS, cols // 128, DEPTH, 2, 128), BF16),
            pltpu.VMEM((2 * rows, 2 * local), BF16),
            pltpu.VMEM((tensors, rows, local), BF16),
            pltpu.VMEM((high, local // CUT), BF16),
            pltpu.VMEM((high, local // CUT), BF16),
            pltpu.VMEM((tensors, adapters * MOST, 128), F32),
            pltpu.VMEM((high, cols), BF16),
            pltpu.VMEM((high, cols), BF16),
            pltpu.VMEM(down.shape[1:], BF16),
            pltpu.VMEM(up.shape[1:], BF16),
            pltpu.VMEM((2 * rows, cols), F32),
            dma((SLOTS, cols // 128)),
            dma((2,)),
            dma((tensors,)), dma((tensors,)),
            dma((adapters,)), dma((adapters,)),
            dma((tensors,)), dma((tensors,)),
            dma((adapters,)), dma((adapters,)),
        ],
        compiler_params=pltpu.CompilerParams(
            collective_id=0, has_side_effects=True, vmem_limit_bytes=40 << 20
        ),
        name="entries",
    )(hidden, weight, down, up, index, index.reshape(1, rows), cosine, sine)


def attend_kernel(lengths, queries, cache, entries, out, held, sems):
    requests, lines, _ = queries.shape
    context = cache.shape[2]
    heads = lines // GROUP
    chunks = context // CHUNK
    scaling = HEAD_DIM ** -0.5

    def copies(r, act):
        slot = lax.rem(r, AHEAD)
        for c in range(chunks):
            @pl.when(c * CHUNK < lengths[r])
            def _():
                act(
                    pltpu.make_async_copy(
                        cache.at[r, :, pl.ds(c * CHUNK, CHUNK), :],
                        held.at[slot, :, pl.ds(c * CHUNK, CHUNK), :],
                        sems.at[slot, c],
                    )
                )

    for r in range(AHEAD):
        copies(r, lambda copy: copy.start())

    owner = iota((lines, HEAD_DIM), 0) // GROUP

    def own(fields):
        chosen = jnp.zeros((lines, HEAD_DIM), F32)
        for head in range(heads):
            part = fields[:, head * HEAD_DIM : (head + 1) * HEAD_DIM]
            chosen = jnp.where(owner == head, part, chosen)
        return chosen

    def step(r, carry):
        slot = lax.rem(r, AHEAD)
        copies(r, lambda copy: copy.wait())
        length = lengths[r]
        query = queries[r]
        apart = jnp.concatenate(
            [jnp.where(owner == head, query, 0).astype(BF16) for head in range(heads)], 1
        )
        own_score = jnp.sum(
            query.astype(F32) * own(entries[0, pl.ds(r, 1), :]), axis=1, keepdims=True
        ) * scaling
        own_value = own(entries[1, pl.ds(r, 1), :])

        for used in range(1, chunks + 1):
            @pl.when((length > (used - 1) * CHUNK) & (length <= used * CHUNK))
            def _():
                size = used * CHUNK
                scores = lax.dot_general(
                    apart, held[slot, 0, :size, :], (((1,), (1,)), ((), ())),
                    preferred_element_type=F32,
                ) * scaling
                valid = iota((lines, size), 1) < length
                scores = jnp.where(valid, scores, -1e30)
                highest = jnp.maximum(jnp.max(scores, axis=1, keepdims=True), own_score)
                weights = jnp.where(valid, jnp.exp(scores - highest), 0.0)
                own_weight = jnp.exp(own_score - highest)
                inverse = 1.0 / (jnp.sum(weights, axis=1, keepdims=True) + own_weight)
                probs = (weights * inverse).astype(BF16)
                own_prob = (own_weight * inverse).astype(BF16).astype(F32)
                mixed = own(
                    jnp.dot(probs, held[slot, 1, :size, :], preferred_element_type=F32)
                )
                out[r] = (mixed + own_prob * own_value).astype(BF16)

        @pl.when(r + AHEAD < requests)
        def _():
            copies(r + AHEAD, lambda copy: copy.start())

        return carry

    lax.fori_loop(0, requests, step, 0)


def attend(lengths, queries, cache, entries):
    requests, _, context, cols = cache.shape
    vmem = pl.BlockSpec(memory_space=pltpu.VMEM)
    return pl.pallas_call(
        attend_kernel,
        out_shape=jax.ShapeDtypeStruct(queries.shape, BF16),
        in_specs=[
            pl.BlockSpec(memory_space=pltpu.SMEM), vmem, pl.BlockSpec(memory_space=pl.ANY), vmem
        ],
        out_specs=vmem,
        scratch_shapes=[
            pltpu.VMEM((AHEAD, 2, context, cols), BF16),
            pltpu.SemaphoreType.DMA((AHEAD, context // CHUNK)),
        ],
        compiler_params=pltpu.CompilerParams(vmem_limit_bytes=40 << 20),
        name="attend",
    )(lengths, queries, cache, entries)


def on_device(
    adapters, tensors,
    hidden, queries, key_value_cache, key_value_weight,
    adapter_down_weight, adapter_up_weight, request_adapter_index, lengths,
):
    requests = hidden.shape[0]
    half = HEAD_DIM // 2
    freqs = THETA ** (-(jnp.arange(half, dtype=F32) * 2.0) / HEAD_DIM)
    angles = lengths.astype(F32)[:, None] * freqs[None, :]
    cosine = jnp.concatenate([jnp.cos(angles)] * 2, -1)
    sine = jnp.sin(angles)
    sine = jnp.concatenate([-sine, sine], -1)
    entries = entries_of(
        adapters, tensors, hidden, key_value_weight, adapter_down_weight, adapter_up_weight,
        request_adapter_index, cosine, sine,
    )
    attention = attend(
        lengths, queries.reshape(requests, -1, HEAD_DIM), key_value_cache, entries
    )
    return (
        attention.reshape(requests, -1),
        jnp.swapaxes(entries, 0, 1).astype(BF16),
    )


def solution(mesh):
    in_specs = (
        P(("groups", "adapt"), "tensor"),
        P(("groups", "adapt"), "tensor"),
        P(("groups", "adapt"), None, None, "tensor"),
        P(None, None, "tensor"),
        P("adapt", "tensor", None),
        P("adapt", None, None, "tensor"),
        P(("groups", "adapt"), None),
        P(("groups", "adapt")),
    )
    out_specs = (P(("groups", "adapt"), "tensor"), P(("groups", "adapt"), None, "tensor"))
    return jax.shard_map(
        functools.partial(on_device, mesh.shape["adapt"], mesh.shape["tensor"]),
        mesh=mesh, in_specs=in_specs, out_specs=out_specs, check_vma=False,
    )
```

```python
import functools

import jax
import jax.numpy as jnp
from jax import lax
from jax.experimental import pallas as pl
from jax.experimental.pallas import tpu as pltpu
from jax.sharding import PartitionSpec as P

HEAD_DIM = 128
GROUP = 8
MOST = 4
ADAPTER_SCALE = 2.0
THETA = 500000.0
ROWS = 16
CUT = ROWS // MOST
DEPTH = 512
SLOTS = 4
CHUNK = 128
AHEAD = 16
TOGETHER = 4
MESH = pl.DeviceIdType.MESH
F32 = jnp.float32
BF16 = jnp.bfloat16


def one_hot(condition):
    return jnp.where(condition, 1.0, 0.0).astype(BF16)


def iota(shape, dim):
    return lax.broadcasted_iota(jnp.int32, shape, dim)


def entries_kernel(
    adapters, tensors,
    hidden, weight, down, up, index_col, index_row, cosine, sine, out,
    blocks, wide, gathered, sent, taken, partial, back_sent, back, down_here, up_here, total,
    block_sem, local_sem, hs, hr, ds, dr, ps, pr, rs, rr,
):
    me = lax.axis_index("adapt")
    side = lax.axis_index("tensor")
    rows, local = hidden.shape
    cols = out.shape[2]
    tiles = cols // 128
    per_source = local // DEPTH
    count = per_source * tensors
    piece = local // CUT

    def block_copies(n):
        source = lax.rem(side + tensors - n // per_source, tensors)
        start = pl.multiple_of(source * local + lax.rem(n, per_source) * DEPTH, DEPTH)
        slot = lax.rem(n, SLOTS)
        return [
            pltpu.make_async_copy(
                weight.at[pl.ds(start, DEPTH), :, pl.ds(tile * 128, 128)],
                blocks.at[slot, tile],
                block_sem.at[slot, tile],
            )
            for tile in range(tiles)
        ]

    down_copy = pltpu.make_async_copy(down.at[0], down_here, local_sem.at[0])
    up_copy = pltpu.make_async_copy(up.at[0], up_here, local_sem.at[1])

    barrier = pltpu.get_barrier_semaphore()
    for j in range(1, adapters):
        pl.semaphore_signal(
            barrier, inc=1, device_id={"adapt": lax.rem(me + j, adapters)}, device_id_type=MESH
        )
    for j in range(1, tensors):
        pl.semaphore_signal(
            barrier, inc=1, device_id={"tensor": lax.rem(side + j, tensors)}, device_id_type=MESH
        )
    for n in range(SLOTS):
        for copy in block_copies(jnp.int32(n)):
            copy.start()
    down_copy.start()
    up_copy.start()

    col = index_col[...]
    row = index_row[...]
    same = col == row
    first, second = iota((rows, rows), 0), iota((rows, rows), 1)
    place_col = jnp.sum(jnp.where(same & (second < first), 1.0, 0.0), axis=1, keepdims=True)
    place_row = jnp.sum(jnp.where(same & (first < second), 1.0, 0.0), axis=0, keepdims=True)
    place_col = place_col.astype(jnp.int32)
    place_row = place_row.astype(jnp.int32)

    high = adapters * ROWS
    line = iota((high, rows), 0)
    wanted = (line // ROWS == row) & (line % MOST == place_row)
    packed = jnp.zeros((high, piece), F32)
    for q in range(CUT):
        pick = one_hot(wanted & (line % ROWS // MOST == q))
        packed += jnp.dot(
            pick, hidden[:, q * piece : (q + 1) * piece], preferred_element_type=F32
        )
    sent[...] = packed.astype(BF16)
    here = pl.ds(pl.multiple_of(me * ROWS, ROWS), ROWS)

    pl.semaphore_wait(barrier, adapters - 1 + tensors - 1)

    def block_of(j):
        return pl.ds(pl.multiple_of(lax.rem(me + j, adapters) * ROWS, ROWS), ROWS)

    out_copies, back_copies = [None], [None]
    for j in range(1, adapters):
        copy = pltpu.make_async_remote_copy(
            src_ref=sent.at[block_of(j)],
            dst_ref=taken.at[here],
            send_sem=ds.at[j],
            recv_sem=dr.at[j],
            device_id={"adapt": lax.rem(me + j, adapters)},
            device_id_type=MESH,
        )
        copy.start()
        out_copies.append(copy)
    hidden_copies, sum_copies = [None], [None]
    for j in range(1, tensors):
        copy = pltpu.make_async_remote_copy(
            src_ref=hidden,
            dst_ref=gathered.at[j],
            send_sem=hs.at[j],
            recv_sem=hr.at[j],
            device_id={"tensor": lax.rem(side + j, tensors)},
            device_id_type=MESH,
        )
        copy.start()
        hidden_copies.append(copy)
    taken[here] = sent[here]
    total[...] = jnp.zeros_like(total)

    spread = iota((128, 256), 1) - 2 * iota((128, 256), 0)
    even, odd = one_hot(spread == 0), one_hot(spread == 1)

    def widen(source):
        for at in range(local // 128):
            part = source[:, at * 128 : (at + 1) * 128]
            to = slice(at * 256, (at + 1) * 256)
            wide[:rows, to] = jnp.dot(part, even, preferred_element_type=F32).astype(BF16)
            wide[rows:, to] = jnp.dot(part, odd, preferred_element_type=F32).astype(BF16)

    def stream(low, top):
        def step(n, carry):
            slot = lax.rem(n, SLOTS)
            start = pl.multiple_of(lax.rem(n, per_source) * 2 * DEPTH, 2 * DEPTH)
            features = wide[:, pl.ds(start, 2 * DEPTH)]
            for tile, copy in enumerate(block_copies(n)):
                copy.wait()
                total[:, tile * 128 : (tile + 1) * 128] += jnp.dot(
                    features,
                    blocks.at[slot, tile].reshape(2 * DEPTH, 128)[...],
                    preferred_element_type=F32,
                )

            @pl.when(n + SLOTS < count)
            def _():
                for copy in block_copies(n + SLOTS):
                    copy.start()

            return carry

        lax.fori_loop(low, top, step, 0)

    widen(hidden)
    stream(0, per_source)

    for j in range(1, adapters):
        out_copies[j].wait_recv()
    down_copy.wait()
    arrived = taken[...]
    which = iota((high, 128), 0) % ROWS // MOST
    grown = jnp.zeros((high, 128), F32)
    for q in range(CUT):
        product = jnp.dot(
            arrived, down_here[q * piece : (q + 1) * piece, :], preferred_element_type=F32
        )
        grown = jnp.where(which == q, product, grown)
    short = adapters * MOST
    to, fro = iota((short, high), 0), iota((short, high), 1)
    fold = (to // MOST == fro // ROWS) & (to % MOST == fro % MOST)
    partial[0] = jnp.dot(
        jnp.where(fold, 1.0, 0.0), grown,
        preferred_element_type=F32, precision=lax.Precision.HIGHEST,
    )
    for j in range(1, tensors):
        copy = pltpu.make_async_remote_copy(
            src_ref=partial.at[0],
            dst_ref=partial.at[j],
            send_sem=ps.at[j],
            recv_sem=pr.at[j],
            device_id={"tensor": lax.rem(side + j, tensors)},
            device_id_type=MESH,
        )
        copy.start()
        sum_copies.append(copy)

    hidden_copies[1].wait_recv()
    widen(gathered.at[1])
    middle = per_source + per_source // 2
    stream(per_source, middle)

    up_copy.wait()
    rank_sum = partial[0]
    for j in range(1, tensors):
        sum_copies[j].wait_recv()
        rank_sum = rank_sum + partial[j]
    shrunk = rank_sum.astype(BF16)
    half = up_here.shape[1]
    to, fro = iota((high, short), 0), iota((high, short), 1)
    returned = jnp.zeros((high, cols), F32)
    for t in range(2):
        raised = jnp.dot(
            shrunk[:, t * half : (t + 1) * half], up_here[t], preferred_element_type=F32
        )
        raised = (ADAPTER_SCALE * raised).astype(BF16)
        put = (to // ROWS == fro // MOST) & (to % ROWS == fro % MOST + t * MOST)
        returned += jnp.dot(one_hot(put), raised, preferred_element_type=F32)
    back_sent[...] = returned.astype(BF16)
    for j in range(1, adapters):
        copy = pltpu.make_async_remote_copy(
            src_ref=back_sent.at[block_of(j)],
            dst_ref=back.at[here],
            send_sem=rs.at[j],
            recv_sem=rr.at[j],
            device_id={"adapt": lax.rem(me + j, adapters)},
            device_id_type=MESH,
        )
        copy.start()
        back_copies.append(copy)
    back[here] = back_sent[here]

    stream(middle, 2 * per_source)
    for j in range(2, tensors):
        hidden_copies[j].wait_recv()
        widen(gathered.at[j])
        stream(j * per_source, (j + 1) * per_source)

    for j in range(1, adapters):
        back_copies[j].wait_recv()
    updates = back[...]
    line = iota((rows, high), 1)
    for t in range(2):
        choose = one_hot((line // ROWS == col) & (line % ROWS == place_col + t * MOST))
        fresh = total[t * rows : (t + 1) * rows, :] + jnp.dot(
            choose, updates, preferred_element_type=F32
        )
        for head in range(cols // HEAD_DIM):
            at = slice(head * HEAD_DIM, (head + 1) * HEAD_DIM)
            part = fresh[:, at]
            if t == 0:
                part = part * cosine[...] + pltpu.roll(part, HEAD_DIM // 2, 1) * sine[...]
            out[t, :, at] = part.astype(BF16).astype(F32)

    for j in range(1, adapters):
        out_copies[j].wait_send()
        back_copies[j].wait_send()
    for j in range(1, tensors):
        hidden_copies[j].wait_send()
        sum_copies[j].wait_send()


def entries_of(adapters, tensors, hidden, weight, down, up, index, cosine, sine):
    rows, local = hidden.shape
    cols = weight.shape[2]
    high = adapters * ROWS
    dma = pltpu.SemaphoreType.DMA
    vmem = pl.BlockSpec(memory_space=pltpu.VMEM)
    hbm = pl.BlockSpec(memory_space=pl.ANY)
    return pl.pallas_call(
        functools.partial(entries_kernel, adapters, tensors),
        out_shape=jax.ShapeDtypeStruct((2, rows, cols), F32),
        in_specs=[vmem, hbm, hbm, hbm, vmem, vmem, vmem, vmem],
        out_specs=vmem,
        scratch_shapes=[
            pltpu.VMEM((SLOTS, cols // 128, DEPTH, 2, 128), BF16),
            pltpu.VMEM((2 * rows, 2 * local), BF16),
            pltpu.VMEM((tensors, rows, local), BF16),
            pltpu.VMEM((high, local // CUT), BF16),
            pltpu.VMEM((high, local // CUT), BF16),
            pltpu.VMEM((tensors, adapters * MOST, 128), F32),
            pltpu.VMEM((high, cols), BF16),
            pltpu.VMEM((high, cols), BF16),
            pltpu.VMEM(down.shape[1:], BF16),
            pltpu.VMEM(up.shape[1:], BF16),
            pltpu.VMEM((2 * rows, cols), F32),
            dma((SLOTS, cols // 128)),
            dma((2,)),
            dma((tensors,)), dma((tensors,)),
            dma((adapters,)), dma((adapters,)),
            dma((tensors,)), dma((tensors,)),
            dma((adapters,)), dma((adapters,)),
        ],
        compiler_params=pltpu.CompilerParams(
            collective_id=0, has_side_effects=True, vmem_limit_bytes=40 << 20
        ),
        name="entries",
    )(hidden, weight, down, up, index, index.reshape(1, rows), cosine, sine)


def attend_kernel(lengths, queries, cache, entries, out, held, sems):
    requests, lines, _ = queries.shape
    context, cols = cache.shape[2:]
    heads = lines // GROUP
    chunks = context // CHUNK
    scaling = HEAD_DIM ** -0.5

    def copies(r, act):
        slot = lax.rem(r, AHEAD)
        for c in range(chunks):
            @pl.when(c * CHUNK < lengths[r])
            def _():
                act(
                    pltpu.make_async_copy(
                        cache.at[r, :, pl.ds(c * CHUNK, CHUNK), :],
                        held.at[slot, :, pl.ds(c * CHUNK, CHUNK), :],
                        sems.at[slot, c],
                    )
                )

    for r in range(AHEAD):
        copies(r, lambda copy: copy.start())
        for c in range(chunks):
            @pl.when(c * CHUNK >= lengths[r])
            def _():
                held[r, 1, c * CHUNK : (c + 1) * CHUNK, :] = jnp.zeros((CHUNK, cols), BF16)

    owner = iota((lines, HEAD_DIM), 0) // GROUP

    def own(fields):
        chosen = jnp.zeros((lines, HEAD_DIM), F32)
        for head in range(heads):
            part = fields[:, head * HEAD_DIM : (head + 1) * HEAD_DIM]
            chosen = jnp.where(owner == head, part, chosen)
        return chosen

    def one(r):
        slot = lax.rem(r, AHEAD)
        length = lengths[r]
        query = queries[r]
        apart = jnp.concatenate(
            [jnp.where(owner == head, query, 0).astype(BF16) for head in range(heads)], 1
        )
        own_score = jnp.sum(
            query.astype(F32) * own(entries[0, pl.ds(r, 1), :]), axis=1, keepdims=True
        ) * scaling
        scores = lax.dot_general(
            apart, held[slot, 0], (((1,), (1,)), ((), ())), preferred_element_type=F32
        ) * scaling
        valid = iota((lines, context), 1) < length
        scores = jnp.where(valid, scores, -1e30)
        highest = jnp.maximum(jnp.max(scores, axis=1, keepdims=True), own_score)
        weights = jnp.where(valid, jnp.exp(scores - highest), 0.0)
        own_weight = jnp.exp(own_score - highest)
        inverse = 1.0 / (jnp.sum(weights, axis=1, keepdims=True) + own_weight)
        probs = (weights * inverse).astype(BF16)
        own_prob = (own_weight * inverse).astype(BF16).astype(F32)
        mixed = own(jnp.dot(probs, held[slot, 1], preferred_element_type=F32))
        return (mixed + own_prob * own(entries[1, pl.ds(r, 1), :])).astype(BF16)

    def step(n, carry):
        base = n * TOGETHER
        for k in range(TOGETHER):
            copies(base + k, lambda copy: copy.wait())
        results = [one(base + k) for k in range(TOGETHER)]
        for k in range(TOGETHER):
            out[base + k] = results[k]
        for k in range(TOGETHER):
            @pl.when(base + k + AHEAD < requests)
            def _():
                copies(base + k + AHEAD, lambda copy: copy.start())

        return carry

    lax.fori_loop(0, requests // TOGETHER, step, 0)


def attend(lengths, queries, cache, entries):
    requests, _, context, cols = cache.shape
    vmem = pl.BlockSpec(memory_space=pltpu.VMEM)
    return pl.pallas_call(
        attend_kernel,
        out_shape=jax.ShapeDtypeStruct(queries.shape, BF16),
        in_specs=[
            pl.BlockSpec(memory_space=pltpu.SMEM), vmem, pl.BlockSpec(memory_space=pl.ANY), vmem
        ],
        out_specs=vmem,
        scratch_shapes=[
            pltpu.VMEM((AHEAD, 2, context, cols), BF16),
            pltpu.SemaphoreType.DMA((AHEAD, context // CHUNK)),
        ],
        compiler_params=pltpu.CompilerParams(vmem_limit_bytes=40 << 20),
        name="attend",
    )(lengths, queries, cache, entries)


def on_device(
    adapters, tensors,
    hidden, queries, key_value_cache, key_value_weight,
    adapter_down_weight, adapter_up_weight, request_adapter_index, lengths,
):
    requests = hidden.shape[0]
    half = HEAD_DIM // 2
    freqs = THETA ** (-(jnp.arange(half, dtype=F32) * 2.0) / HEAD_DIM)
    angles = lengths.astype(F32)[:, None] * freqs[None, :]
    cosine = jnp.concatenate([jnp.cos(angles)] * 2, -1)
    sine = jnp.sin(angles)
    sine = jnp.concatenate([-sine, sine], -1)
    entries = entries_of(
        adapters, tensors, hidden, key_value_weight, adapter_down_weight, adapter_up_weight,
        request_adapter_index, cosine, sine,
    )
    attention = attend(
        lengths, queries.reshape(requests, -1, HEAD_DIM), key_value_cache, entries
    )
    return (
        attention.reshape(requests, -1),
        jnp.swapaxes(entries, 0, 1).astype(BF16),
    )


def solution(mesh):
    in_specs = (
        P(("groups", "adapt"), "tensor"),
        P(("groups", "adapt"), "tensor"),
        P(("groups", "adapt"), None, None, "tensor"),
        P(None, None, "tensor"),
        P("adapt", "tensor", None),
        P("adapt", None, None, "tensor"),
        P(("groups", "adapt"), None),
        P(("groups", "adapt")),
    )
    out_specs = (P(("groups", "adapt"), "tensor"), P(("groups", "adapt"), None, "tensor"))
    return jax.shard_map(
        functools.partial(on_device, mesh.shape["adapt"], mesh.shape["tensor"]),
        mesh=mesh, in_specs=in_specs, out_specs=out_specs, check_vma=False,
    )
```

```python
import functools

import jax
import jax.numpy as jnp
from jax import lax
from jax.experimental import pallas as pl
from jax.experimental.pallas import tpu as pltpu
from jax.sharding import PartitionSpec as P

HEAD_DIM = 128
GROUP = 8
MOST = 4
ADAPTER_SCALE = 2.0
THETA = 500000.0
ROWS = 16
CUT = ROWS // MOST
DEPTH = 512
SLOTS = 4
CHUNK = 128
AHEAD = 16
TOGETHER = 4
MESH = pl.DeviceIdType.MESH
F32 = jnp.float32
BF16 = jnp.bfloat16


def one_hot(condition):
    return jnp.where(condition, 1.0, 0.0).astype(BF16)


def iota(shape, dim):
    return lax.broadcasted_iota(jnp.int32, shape, dim)


def entries_kernel(
    adapters, tensors,
    hidden, weight, down, up, index_col, index_row, cosine, sine, out,
    blocks, wide, gathered, sent, taken, partial, back_sent, back, down_here, up_here, total,
    block_sem, local_sem, hs, hr, ds, dr, ps, pr, rs, rr,
):
    me = lax.axis_index("adapt")
    side = lax.axis_index("tensor")
    rows, local = hidden.shape
    cols = out.shape[2]
    tiles = cols // 128
    per_source = local // DEPTH
    count = per_source * tensors
    piece = local // CUT

    def block_copies(n):
        source = lax.rem(side + tensors - n // per_source, tensors)
        start = pl.multiple_of(source * local + lax.rem(n, per_source) * DEPTH, DEPTH)
        slot = lax.rem(n, SLOTS)
        return [
            pltpu.make_async_copy(
                weight.at[pl.ds(start, DEPTH), :, pl.ds(tile * 128, 128)],
                blocks.at[slot, tile],
                block_sem.at[slot, tile],
            )
            for tile in range(tiles)
        ]

    down_copy = pltpu.make_async_copy(down.at[0], down_here, local_sem.at[0])
    up_copy = pltpu.make_async_copy(up.at[0], up_here, local_sem.at[1])

    barrier = pltpu.get_barrier_semaphore()
    for j in range(1, adapters):
        pl.semaphore_signal(
            barrier, inc=1, device_id={"adapt": lax.rem(me + j, adapters)}, device_id_type=MESH
        )
    for j in range(1, tensors):
        pl.semaphore_signal(
            barrier, inc=1, device_id={"tensor": lax.rem(side + j, tensors)}, device_id_type=MESH
        )
    for n in range(SLOTS):
        for copy in block_copies(jnp.int32(n)):
            copy.start()
    down_copy.start()
    up_copy.start()

    col = index_col[...]
    row = index_row[...]
    same = col == row
    first, second = iota((rows, rows), 0), iota((rows, rows), 1)
    place_col = jnp.sum(jnp.where(same & (second < first), 1.0, 0.0), axis=1, keepdims=True)
    place_row = jnp.sum(jnp.where(same & (first < second), 1.0, 0.0), axis=0, keepdims=True)
    place_col = place_col.astype(jnp.int32)
    place_row = place_row.astype(jnp.int32)

    high = adapters * ROWS
    line = iota((high, rows), 0)
    wanted = (line // ROWS == row) & (line % MOST == place_row)
    packed = jnp.zeros((high, piece), F32)
    for q in range(CUT):
        pick = one_hot(wanted & (line % ROWS // MOST == q))
        packed += jnp.dot(
            pick, hidden[:, q * piece : (q + 1) * piece], preferred_element_type=F32
        )
    sent[...] = packed.astype(BF16)
    here = pl.ds(pl.multiple_of(me * ROWS, ROWS), ROWS)

    pl.semaphore_wait(barrier, adapters - 1 + tensors - 1)

    def block_of(j):
        return pl.ds(pl.multiple_of(lax.rem(me + j, adapters) * ROWS, ROWS), ROWS)

    out_copies, back_copies = [None], [None]
    for j in range(1, adapters):
        copy = pltpu.make_async_remote_copy(
            src_ref=sent.at[block_of(j)],
            dst_ref=taken.at[here],
            send_sem=ds.at[j],
            recv_sem=dr.at[j],
            device_id={"adapt": lax.rem(me + j, adapters)},
            device_id_type=MESH,
        )
        copy.start()
        out_copies.append(copy)
    hidden_copies, sum_copies = [None], [None]
    for j in range(1, tensors):
        copy = pltpu.make_async_remote_copy(
            src_ref=hidden,
            dst_ref=gathered.at[j],
            send_sem=hs.at[j],
            recv_sem=hr.at[j],
            device_id={"tensor": lax.rem(side + j, tensors)},
            device_id_type=MESH,
        )
        copy.start()
        hidden_copies.append(copy)
    taken[here] = sent[here]
    total[...] = jnp.zeros_like(total)

    spread = iota((128, 256), 1) - 2 * iota((128, 256), 0)
    even, odd = one_hot(spread == 0), one_hot(spread == 1)

    def widen(source):
        for at in range(local // 128):
            part = source[:, at * 128 : (at + 1) * 128]
            to = slice(at * 256, (at + 1) * 256)
            wide[:rows, to] = jnp.dot(part, even, preferred_element_type=F32).astype(BF16)
            wide[rows:, to] = jnp.dot(part, odd, preferred_element_type=F32).astype(BF16)

    def stream(low, top):
        def step(n, carry):
            slot = lax.rem(n, SLOTS)
            start = pl.multiple_of(lax.rem(n, per_source) * 2 * DEPTH, 2 * DEPTH)
            features = wide[:, pl.ds(start, 2 * DEPTH)]
            for copy in block_copies(n):
                copy.wait()
            for tile in range(tiles):
                total[:, tile * 128 : (tile + 1) * 128] += jnp.dot(
                    features,
                    blocks.at[slot, tile].reshape(2 * DEPTH, 128)[...],
                    preferred_element_type=F32,
                )

            @pl.when(n + SLOTS < count)
            def _():
                for copy in block_copies(n + SLOTS):
                    copy.start()

            return carry

        lax.fori_loop(low, top, step, 0)

    widen(hidden)
    stream(0, per_source)

    for j in range(1, adapters):
        out_copies[j].wait_recv()
    down_copy.wait()
    arrived = taken[...]
    which = iota((high, 128), 0) % ROWS // MOST
    grown = jnp.zeros((high, 128), F32)
    for q in range(CUT):
        product = jnp.dot(
            arrived, down_here[q * piece : (q + 1) * piece, :], preferred_element_type=F32
        )
        grown = jnp.where(which == q, product, grown)
    short = adapters * MOST
    to, fro = iota((short, high), 0), iota((short, high), 1)
    fold = (to // MOST == fro // ROWS) & (to % MOST == fro % MOST)
    partial[0] = jnp.dot(
        jnp.where(fold, 1.0, 0.0), grown,
        preferred_element_type=F32, precision=lax.Precision.HIGHEST,
    )
    for j in range(1, tensors):
        copy = pltpu.make_async_remote_copy(
            src_ref=partial.at[0],
            dst_ref=partial.at[j],
            send_sem=ps.at[j],
            recv_sem=pr.at[j],
            device_id={"tensor": lax.rem(side + j, tensors)},
            device_id_type=MESH,
        )
        copy.start()
        sum_copies.append(copy)

    hidden_copies[1].wait_recv()
    widen(gathered.at[1])
    middle = per_source + per_source // 2
    stream(per_source, middle)

    up_copy.wait()
    rank_sum = partial[0]
    for j in range(1, tensors):
        sum_copies[j].wait_recv()
        rank_sum = rank_sum + partial[j]
    shrunk = rank_sum.astype(BF16)
    half = up_here.shape[1]
    to, fro = iota((high, short), 0), iota((high, short), 1)
    returned = jnp.zeros((high, cols), F32)
    for t in range(2):
        raised = jnp.dot(
            shrunk[:, t * half : (t + 1) * half], up_here[t], preferred_element_type=F32
        )
        raised = (ADAPTER_SCALE * raised).astype(BF16)
        put = (to // ROWS == fro // MOST) & (to % ROWS == fro % MOST + t * MOST)
        returned += jnp.dot(one_hot(put), raised, preferred_element_type=F32)
    back_sent[...] = returned.astype(BF16)
    for j in range(1, adapters):
        copy = pltpu.make_async_remote_copy(
            src_ref=back_sent.at[block_of(j)],
            dst_ref=back.at[here],
            send_sem=rs.at[j],
            recv_sem=rr.at[j],
            device_id={"adapt": lax.rem(me + j, adapters)},
            device_id_type=MESH,
        )
        copy.start()
        back_copies.append(copy)
    back[here] = back_sent[here]

    stream(middle, 2 * per_source)
    for j in range(2, tensors):
        hidden_copies[j].wait_recv()
        widen(gathered.at[j])
        stream(j * per_source, (j + 1) * per_source)

    for j in range(1, adapters):
        back_copies[j].wait_recv()
    updates = back[...]
    line = iota((rows, high), 1)
    for t in range(2):
        choose = one_hot((line // ROWS == col) & (line % ROWS == place_col + t * MOST))
        fresh = total[t * rows : (t + 1) * rows, :] + jnp.dot(
            choose, updates, preferred_element_type=F32
        )
        for head in range(cols // HEAD_DIM):
            at = slice(head * HEAD_DIM, (head + 1) * HEAD_DIM)
            part = fresh[:, at]
            if t == 0:
                part = part * cosine[...] + pltpu.roll(part, HEAD_DIM // 2, 1) * sine[...]
            out[t, :, at] = part.astype(BF16).astype(F32)

    for j in range(1, adapters):
        out_copies[j].wait_send()
        back_copies[j].wait_send()
    for j in range(1, tensors):
        hidden_copies[j].wait_send()
        sum_copies[j].wait_send()


def entries_of(adapters, tensors, hidden, weight, down, up, index, cosine, sine):
    rows, local = hidden.shape
    cols = weight.shape[2]
    high = adapters * ROWS
    dma = pltpu.SemaphoreType.DMA
    vmem = pl.BlockSpec(memory_space=pltpu.VMEM)
    hbm = pl.BlockSpec(memory_space=pl.ANY)
    return pl.pallas_call(
        functools.partial(entries_kernel, adapters, tensors),
        out_shape=jax.ShapeDtypeStruct((2, rows, cols), F32),
        in_specs=[vmem, hbm, hbm, hbm, vmem, vmem, vmem, vmem],
        out_specs=vmem,
        scratch_shapes=[
            pltpu.VMEM((SLOTS, cols // 128, DEPTH, 2, 128), BF16),
            pltpu.VMEM((2 * rows, 2 * local), BF16),
            pltpu.VMEM((tensors, rows, local), BF16),
            pltpu.VMEM((high, local // CUT), BF16),
            pltpu.VMEM((high, local // CUT), BF16),
            pltpu.VMEM((tensors, adapters * MOST, 128), F32),
            pltpu.VMEM((high, cols), BF16),
            pltpu.VMEM((high, cols), BF16),
            pltpu.VMEM(down.shape[1:], BF16),
            pltpu.VMEM(up.shape[1:], BF16),
            pltpu.VMEM((2 * rows, cols), F32),
            dma((SLOTS, cols // 128)),
            dma((2,)),
            dma((tensors,)), dma((tensors,)),
            dma((adapters,)), dma((adapters,)),
            dma((tensors,)), dma((tensors,)),
            dma((adapters,)), dma((adapters,)),
        ],
        compiler_params=pltpu.CompilerParams(
            collective_id=0, has_side_effects=True, vmem_limit_bytes=40 << 20
        ),
        name="entries",
    )(hidden, weight, down, up, index, index.reshape(1, rows), cosine, sine)


def attend_kernel(lengths, queries, cache, entries, out, held, sems):
    requests, lines, _ = queries.shape
    context, cols = cache.shape[2:]
    heads = lines // GROUP
    chunks = context // CHUNK
    scaling = HEAD_DIM ** -0.5

    def copies(r, act):
        slot = lax.rem(r, AHEAD)
        for c in range(chunks):
            @pl.when(c * CHUNK < lengths[r])
            def _():
                act(
                    pltpu.make_async_copy(
                        cache.at[r, :, pl.ds(c * CHUNK, CHUNK), :],
                        held.at[slot, :, pl.ds(c * CHUNK, CHUNK), :],
                        sems.at[slot, c],
                    )
                )

    for r in range(AHEAD):
        copies(r, lambda copy: copy.start())
        for c in range(chunks):
            @pl.when(c * CHUNK >= lengths[r])
            def _():
                held[r, 1, c * CHUNK : (c + 1) * CHUNK, :] = jnp.zeros((CHUNK, cols), BF16)

    owner = iota((lines, HEAD_DIM), 0) // GROUP

    def own(fields):
        chosen = jnp.zeros((lines, HEAD_DIM), F32)
        for head in range(heads):
            part = fields[:, head * HEAD_DIM : (head + 1) * HEAD_DIM]
            chosen = jnp.where(owner == head, part, chosen)
        return chosen

    def one(r):
        slot = lax.rem(r, AHEAD)
        length = lengths[r]
        query = queries[r]
        apart = jnp.concatenate(
            [jnp.where(owner == head, query, 0).astype(BF16) for head in range(heads)], 1
        )
        own_score = jnp.sum(
            query.astype(F32) * own(entries[0, pl.ds(r, 1), :]), axis=1, keepdims=True
        ) * scaling
        scores = lax.dot_general(
            apart, held[slot, 0], (((1,), (1,)), ((), ())), preferred_element_type=F32
        ) * scaling
        valid = iota((lines, context), 1) < length
        scores = jnp.where(valid, scores, -1e30)
        highest = jnp.maximum(jnp.max(scores, axis=1, keepdims=True), own_score)
        weights = jnp.where(valid, jnp.exp(scores - highest), 0.0)
        own_weight = jnp.exp(own_score - highest)
        inverse = 1.0 / (jnp.sum(weights, axis=1, keepdims=True) + own_weight)
        probs = (weights * inverse).astype(BF16)
        own_prob = (own_weight * inverse).astype(BF16).astype(F32)
        mixed = own(jnp.dot(probs, held[slot, 1], preferred_element_type=F32))
        return (mixed + own_prob * own(entries[1, pl.ds(r, 1), :])).astype(BF16)

    def step(n, carry):
        base = n * TOGETHER
        for k in range(TOGETHER):
            copies(base + k, lambda copy: copy.wait())
        results = [one(base + k) for k in range(TOGETHER)]
        for k in range(TOGETHER):
            out[base + k] = results[k]
        for k in range(TOGETHER):
            @pl.when(base + k + AHEAD < requests)
            def _():
                copies(base + k + AHEAD, lambda copy: copy.start())

        return carry

    lax.fori_loop(0, requests // TOGETHER, step, 0)


def attend(lengths, queries, cache, entries):
    requests, _, context, cols = cache.shape
    vmem = pl.BlockSpec(memory_space=pltpu.VMEM)
    return pl.pallas_call(
        attend_kernel,
        out_shape=jax.ShapeDtypeStruct(queries.shape, BF16),
        in_specs=[
            pl.BlockSpec(memory_space=pltpu.SMEM), vmem, pl.BlockSpec(memory_space=pl.ANY), vmem
        ],
        out_specs=vmem,
        scratch_shapes=[
            pltpu.VMEM((AHEAD, 2, context, cols), BF16),
            pltpu.SemaphoreType.DMA((AHEAD, context // CHUNK)),
        ],
        compiler_params=pltpu.CompilerParams(vmem_limit_bytes=40 << 20),
        name="attend",
    )(lengths, queries, cache, entries)


def on_device(
    adapters, tensors,
    hidden, queries, key_value_cache, key_value_weight,
    adapter_down_weight, adapter_up_weight, request_adapter_index, lengths,
):
    requests = hidden.shape[0]
    half = HEAD_DIM // 2
    freqs = THETA ** (-(jnp.arange(half, dtype=F32) * 2.0) / HEAD_DIM)
    angles = lengths.astype(F32)[:, None] * freqs[None, :]
    cosine = jnp.concatenate([jnp.cos(angles)] * 2, -1)
    sine = jnp.sin(angles)
    sine = jnp.concatenate([-sine, sine], -1)
    entries = entries_of(
        adapters, tensors, hidden, key_value_weight, adapter_down_weight, adapter_up_weight,
        request_adapter_index, cosine, sine,
    )
    attention = attend(
        lengths, queries.reshape(requests, -1, HEAD_DIM), key_value_cache, entries
    )
    return (
        attention.reshape(requests, -1),
        jnp.swapaxes(entries, 0, 1).astype(BF16),
    )


def solution(mesh):
    in_specs = (
        P(("groups", "adapt"), "tensor"),
        P(("groups", "adapt"), "tensor"),
        P(("groups", "adapt"), None, None, "tensor"),
        P(None, None, "tensor"),
        P("adapt", "tensor", None),
        P("adapt", None, None, "tensor"),
        P(("groups", "adapt"), None),
        P(("groups", "adapt")),
    )
    out_specs = (P(("groups", "adapt"), "tensor"), P(("groups", "adapt"), None, "tensor"))
    return jax.shard_map(
        functools.partial(on_device, mesh.shape["adapt"], mesh.shape["tensor"]),
        mesh=mesh, in_specs=in_specs, out_specs=out_specs, check_vma=False,
    )
```
